32 devices in a mesh: fsdp: 4 (over y, x), context: 2 (over core), expert: 4 (over z).
Axes of the slice: x: 2, y: 2, z: 4, core: 2. Of those that a mesh axis runs over, the one named last changes fastest.
Arguments:
- tokens: bfloat16 [16, 1024, 768], P(('fsdp', 'expert'), 'context'), may hold values from -6 to 6
- cotangent: bfloat16 [16, 1024, 768], P(('fsdp', 'expert'), 'context'), may hold values from -6 to 6
- expert_ids: int32 [16, 1024], P(('fsdp', 'expert'), 'context'), may hold values from 0 to 3, as said below
- capacity_slot: int32 [16, 1024], P(('fsdp', 'expert'), 'context'), may hold values from -1 to 159, as said below
- buckets: int32 [2047], replicated, may hold values from 0 to 31, as said below
- attn_gain: bfloat16 [768], P('fsdp'), may hold values from 0.25 to 1.75
- query_weight: bfloat16 [768, 768], P('fsdp'), may hold values from -0.0390625 to 0.0390625
- key_weight: bfloat16 [768, 768], P('fsdp'), may hold values from -0.21875 to 0.21875
- value_weight: bfloat16 [768, 768], P('fsdp'), may hold values from -0.21875 to 0.21875
- attention_output_matrix: bfloat16 [768, 768], P('fsdp'), may hold values from -2 to 2
- bias_table: bfloat16 [32, 12], P('fsdp'), may hold values from -4 to 4
- mixture_gain: bfloat16 [768], P('fsdp'), may hold values from 0.25 to 1.75
- router_matrix: bfloat16 [768, 4], P('fsdp'), may hold values from -0.15625 to 0.15625
- expert_in: bfloat16 [4, 768, 3072], P('expert', 'fsdp'), may hold values from -0.21875 to 0.21875
- expert_out: bfloat16 [4, 3072, 768], P('expert', 'fsdp'), may hold values from -0.625 to 0.625
Outputs:
- layer_out: bfloat16 [16, 1024, 768], P(('fsdp', 'expert'), 'context')
- tokens_grad: bfloat16 [16, 1024, 768], P(('fsdp', 'expert'), 'context')
- attn_gain_grad: float32 [768], P('fsdp')
- query_grad: float32 [768, 768], P('fsdp')
- key_grad: float32 [768, 768], P('fsdp')
- value_grad: float32 [768, 768], P('fsdp')
- output_grad: float32 [768, 768], P('fsdp')
- bias_grad: float32 [32, 12], P('fsdp')
- mixture_gain_grad: float32 [768], P('fsdp')
- router_grad: float32 [768, 4], P('fsdp')
- expert_in_grad: float32 [4, 768, 3072], P('expert', 'fsdp')
- expert_out_grad: float32 [4, 3072, 768], P('expert', 'fsdp')
The draws below stay inside these ranges and needn't reach their ends.
Inputs may be any that keep to these rules, and one draw needn't show every extreme that they name: `expert_ids`: on every device some expert is named by more than 160 of its 512 tokens. `capacity_slot`: among one device's tokens of one expert, the kept ones hold distinct slots 0 to their count - 1, at most 160 of them; a token is dropped (-1) only where its expert holds 160 kept tokens of that device; on every device some expert fills all 160 slots. Entry j - i + 1023 is the bucket of key j for query i: offsets up to 0 get buckets below 16, positive offsets 32 / 2 and above, never falling as the distance grows on either side.
All inputs are finite; a program needn't handle non-finite values.
Results may differ from the reference program's by a relative error of at most 0.018.
Values may be sent and summed in bfloat16 or wider, within the bound.
A program may use at most 256 MiB of HBM per device.

```python
import jax
import jax.numpy as jnp
from jax import lax

D = 768
HEADS = 12
FF = 3072
BUCKETS = 32
EXP_DEV = 1
SEQ_LEN = 1024
TOK_DEV = 512
SEQS = 16
EXPERTS = 4
CAP = 160


def routing(key):
    expert_groups = EXPERTS // EXP_DEV
    block_count = SEQ_LEN // TOK_DEV
    key_hot, key_base, key_pick, key_order = jax.random.split(key, 4)
    hot_ids = jax.random.randint(key_hot, (SEQS // expert_groups, 1, block_count, 1), 0, EXPERTS)
    hot_ids = jnp.broadcast_to(hot_ids, (SEQS // expert_groups, expert_groups, block_count, TOK_DEV))
    hot_ids = hot_ids.reshape(SEQS, block_count, TOK_DEV)
    base_ids = jax.random.randint(key_base, (SEQS, block_count, TOK_DEV), 0, EXPERTS)
    order_ids = jnp.broadcast_to(jnp.arange(TOK_DEV, dtype=jnp.int32), (SEQS, block_count, TOK_DEV))
    picked = jax.random.permutation(key_pick, order_ids, axis=2, independent=True)
    chosen = jnp.where(picked < CAP + TOK_DEV // 8, hot_ids, base_ids)
    priority = jax.random.permutation(key_order, order_ids, axis=2, independent=True)
    same_expert = chosen[..., :, None] == chosen[..., None, :]
    earlier = priority[..., None, :] < priority[..., :, None]
    rank_ids = jnp.sum((same_expert & earlier).astype(jnp.int32), axis=-1)
    slot_ids = jnp.where(rank_ids < CAP, rank_ids, -1)
    return (chosen.reshape(SEQS, SEQ_LEN), slot_ids.reshape(SEQS, SEQ_LEN))


def draw_expert_ids(key, part):
    return routing(key)[0]


def draw_capacity_slot(key, part):
    return routing(key)[1]


def draw_buckets(key, part):
    key = jax.random.fold_in(key, 5)
    half_count = BUCKETS // 2
    bounds = jnp.sort(jax.random.randint(key, (half_count - 1,), 1, SEQ_LEN))
    offsets = jnp.arange(2 * SEQ_LEN - 1, dtype=jnp.int32) - (SEQ_LEN - 1)
    distance = jnp.abs(offsets)
    levels = jnp.sum((distance[:, None] >= bounds[None, :]).astype(jnp.int32), axis=1)
    return jnp.where(offsets > 0, half_count + levels, levels)


def steps_of(own_key, dims, cuts, low, high):
    gain = 1.0
    for dim, blocks in cuts:
        heights = jax.random.uniform(jax.random.fold_in(jax.random.fold_in(own_key, 6), dim), (blocks,), jnp.float32, low / len(cuts), high / len(cuts))
        gain = gain * jnp.repeat(jnp.exp(heights), dims[dim] // blocks).reshape((-1,) + (1,) * (len(dims) - 1 - dim))
    return gain


def gaussian(own_key, extent, scale, reach, pieces=(), kind=jnp.bfloat16):
    drawn = scale * jax.random.normal(own_key, extent, jnp.float32)
    if pieces:
        drawn = drawn * steps_of(own_key, extent, pieces, -0.22, 0.18)
    return jnp.clip(drawn, -reach, reach).astype(kind)


def setup_inputs(seed: int = 0) -> dict:
    keys = jax.random.split(jax.random.key(seed), 16)
    tokens = gaussian(keys[0], (SEQS, SEQ_LEN, D), 1.0, 6.0, ((0, 16), (1, 2)))
    cotangent = gaussian(keys[1], (SEQS, SEQ_LEN, D), 1.0, 6.0, ((0, 16), (1, 2)))
    expert_ids = draw_expert_ids(jax.random.fold_in(keys[15], 71), 0)
    capacity_slot = draw_capacity_slot(jax.random.fold_in(keys[15], 71), 0)
    buckets = draw_buckets(jax.random.fold_in(keys[15], 71), 0)
    attn_gain = jnp.clip(1.0 + 0.15 * jax.random.normal(keys[5], (D,), jnp.float32), 0.25, 1.75).astype(jnp.bfloat16)
    query_weight = gaussian(keys[6], (D, D), (32 * D) ** -0.5, 0.0390625, ((0, 4),))
    key_weight = gaussian(keys[7], (D, D), D ** -0.5, 0.21875, ((0, 4),))
    value_weight = gaussian(keys[8], (D, D), D ** -0.5, 0.21875, ((0, 4),))
    attention_output_matrix = gaussian(keys[9], (D, D), (max(D // 96, 2)) ** -0.5, 2.0, ((0, 4),))
    bias_table = gaussian(keys[10], (BUCKETS, HEADS), 1.0, 4.0, ((0, 4),))
    mixture_gain = jnp.clip(1.0 + 0.15 * jax.random.normal(keys[11], (D,), jnp.float32), 0.25, 1.75).astype(jnp.bfloat16)
    router_matrix = gaussian(keys[12], (D, EXPERTS), (2 * D) ** -0.5, 0.15625, ((0, 4),))
    expert_in = gaussian(keys[13], (EXPERTS, D, FF), D ** -0.5, 0.21875, ((0, 4), (1, 4)))
    expert_out = gaussian(keys[14], (EXPERTS, FF, D), (FF // 32) ** -0.5, 0.625, ((0, 4), (1, 4)))
    return dict(tokens=tokens, cotangent=cotangent, expert_ids=expert_ids, capacity_slot=capacity_slot, buckets=buckets, attn_gain=attn_gain, query_weight=query_weight, key_weight=key_weight, value_weight=value_weight, attention_output_matrix=attention_output_matrix, bias_table=bias_table, mixture_gain=mixture_gain, router_matrix=router_matrix, expert_in=expert_in, expert_out=expert_out)


@jax.custom_vjp
def low(v):
    return lax.optimization_barrier(v.astype(jnp.bfloat16)).astype(jnp.float32)

@jax.custom_vjp
def low_back(v):
    return v

def low_keep(v):
    return (low(v), None)

def low_pass(kept, grad):
    return (grad,)

def back_keep(v):
    return (v, None)

def back_low(kept, grad):
    return (low(grad),)
low.defvjp(low_keep, low_pass)
low_back.defvjp(back_keep, back_low)
highest_score = lax.Precision.HIGHEST
epsilon = 1e-06

def rms_norm(values, norm_gain):
    return values * lax.rsqrt(lax.optimization_barrier(jnp.mean(values * values, axis=-1, keepdims=True)) + epsilon) * norm_gain

def softmax_last(scores):
    shifted = scores - lax.optimization_barrier(jnp.max(scores, axis=-1, keepdims=True))
    raised = jnp.exp(shifted)
    return raised / lax.optimization_barrier(jnp.sum(raised, axis=-1, keepdims=True))

def attend_one(triple, table_rows, bucket_map):
    query_rows, key_rows, value_rows = triple
    bias_terms = jnp.transpose(jnp.take(table_rows, bucket_map, axis=0), (2, 0, 1))
    scores = jnp.einsum('qhd,khd->hqk', query_rows, key_rows, precision=highest_score) + bias_terms
    scores = low_back(scores)
    weights = low(softmax_last(scores))
    return jnp.einsum('hqk,khd->qhd', weights, value_rows, precision=highest_score)

def forward(inputs, attn_gain, query_weight, key_weight, value_weight, attention_output_matrix, bias_table, mixture_gain, router_matrix, expert_in, expert_out, selector, dispatch, bucket_map):
    seq_count, seq_length, model_width = inputs.shape
    head_count = bias_table.shape[1]
    normalized_input = low(rms_norm(inputs, attn_gain))

    def project(weight_matrix):
        built_output = jnp.einsum('zfv,vh->zfh', normalized_input, weight_matrix, precision=highest_score)
        return low(low_back(built_output)).reshape(seq_count, seq_length, head_count, -1)
    triple = (project(query_weight), project(key_weight), project(value_weight))

    def attend_seq(element):
        return attend_one(element, bias_table, bucket_map)
    attention_result = lax.map(jax.checkpoint(attend_seq), triple)
    attention_result = low(low_back(attention_result.reshape(seq_count, seq_length, model_width)))
    residual_branch = low_back(jnp.einsum('zfv,vh->zfh', attention_result, attention_output_matrix, precision=highest_score))
    middle = inputs + residual_branch
    second_hidden = low(rms_norm(middle, mixture_gain))
    router_logits = jnp.einsum('zfv,vh->zfh', second_hidden, router_matrix, precision=highest_score)
    gate_value = lax.optimization_barrier(jnp.sum(softmax_last(router_logits) * selector, axis=-1))
    blocks = second_hidden.reshape(-1, TOK_DEV, model_width)
    sent = jnp.einsum('btc,btd->bcd', dispatch, blocks, precision=highest_score)
    sent = sent.reshape(-1, EXPERTS, CAP, model_width).transpose(1, 0, 2, 3).reshape(EXPERTS, -1, model_width)
    sent = low_back(sent)
    pre_act = low_back(jnp.einsum('erd,edf->erf', sent, expert_in, precision=highest_score))
    activated = low(jax.nn.gelu(pre_act, approximate=True))
    produced = low(low_back(jnp.einsum('erf,efd->erd', activated, expert_out, precision=highest_score)))
    produced = produced.reshape(EXPERTS, -1, CAP, model_width).transpose(1, 0, 2, 3)
    produced = produced.reshape(-1, EXPERTS * CAP, model_width)
    combined = jnp.einsum('btc,bcd->btd', dispatch, produced, precision=highest_score)
    combined = combined.reshape(seq_count, seq_length, model_width)
    return middle + gate_value[..., None] * combined

def reference(tokens, cotangent, expert_ids, capacity_slot, buckets, attn_gain, query_weight, key_weight, value_weight, attention_output_matrix, bias_table, mixture_gain, router_matrix, expert_in, expert_out):
    selector = (expert_ids[..., None] == jnp.arange(EXPERTS, dtype=jnp.int32)).astype(jnp.float32)
    position = expert_ids * CAP + capacity_slot
    dispatch = (position[..., None] == jnp.arange(EXPERTS * CAP, dtype=jnp.int32)) & (capacity_slot[..., None] >= 0)
    dispatch = dispatch.astype(jnp.float32).reshape(-1, TOK_DEV, EXPERTS * CAP)
    places = jnp.arange(SEQ_LEN, dtype=jnp.int32)
    bucket_map = buckets[places[None, :] - places[:, None] + SEQ_LEN - 1]
    parameters = (attn_gain.astype(jnp.float32), query_weight.astype(jnp.float32), key_weight.astype(jnp.float32), value_weight.astype(jnp.float32), attention_output_matrix.astype(jnp.float32), bias_table.astype(jnp.float32), mixture_gain.astype(jnp.float32), router_matrix.astype(jnp.float32), expert_in.astype(jnp.float32), expert_out.astype(jnp.float32))

    def wrapped(inputs, *weights):
        return forward(inputs, *weights, selector, dispatch, bucket_map)
    result_out, pullback = jax.vjp(wrapped, tokens.astype(jnp.float32), *parameters)
    gradients = pullback(cotangent.astype(jnp.float32))
    return (result_out.astype(jnp.bfloat16), gradients[0].astype(jnp.bfloat16), gradients[1], gradients[2], gradients[3], gradients[4], gradients[5], gradients[6], gradients[7], gradients[8], gradients[9], gradients[10])
```

```python
import functools

import jax
import jax.numpy as jnp
from jax import lax
from jax.experimental import pallas as pl
from jax.experimental.pallas import tpu as pltpu
from jax.sharding import PartitionSpec as P

highest_score = lax.Precision.HIGHEST
epsilon = 1e-06
low = jnp.bfloat16
full = jnp.float32
lane_count = 128


def dot_over(left, right, left_dim, right_dim):
    return lax.dot_general(
        left, right, (((left_dim,), (right_dim,)), ((), ())), preferred_element_type=full
    )


def bias_strip(window):
    width = window.shape[1]
    spread = jnp.broadcast_to(window, (lane_count, width))
    rolled = pltpu.roll(spread, width - lane_count + 1, 1, stride=1, stride_axis=0)
    return rolled[:, : width - lane_count].T


def attention_forward(width, query_ref, key_ref, value_ref, window_ref, out_ref, log_ref, strip_ref):
    queries = query_ref.shape[0]
    keys = key_ref.shape[0]
    per_step = lane_count // width
    tiles = queries // lane_count
    lanes = lax.broadcasted_iota(jnp.int32, (1, lane_count), 1) // width
    rows = lax.broadcasted_iota(jnp.int32, (lane_count, 1), 0) // width
    values_turned = value_ref[...].T
    for head in range(per_step):
        strip_ref[head] = bias_strip(window_ref[head])
    for tile in range(tiles):
        span = pl.ds(tile * lane_count, lane_count)
        query_tile = query_ref[span, :]
        total = jnp.zeros((lane_count, lane_count), full)
        for head in range(per_step):
            own = jnp.where(lanes == head, query_tile, jnp.zeros_like(query_tile))
            scores = dot_over(key_ref[...], own, 1, 1)
            scores = scores + strip_ref[head, pl.ds((tiles - 1 - tile) * lane_count, keys), :]
            top = jnp.max(scores, axis=0, keepdims=True)
            raised = jnp.exp(scores - top)
            summed = jnp.sum(raised, axis=0, keepdims=True)
            log_ref[head, :, span] = top + jnp.log(summed)
            part = dot_over(values_turned, raised.astype(low), 1, 0) / summed
            total = jnp.where(rows == head, part, total)
        out_ref[span, :] = total.T.astype(low)


def diagonal_fold(strip_sum, window_width):
    turned = strip_sum.T
    turned = jnp.concatenate(
        (turned, jnp.zeros((lane_count, window_width - turned.shape[1]), full)), axis=1
    )
    size = lane_count
    while size > 1:
        size //= 2
        turned = pltpu.roll(turned[:size], size, 1) + turned[size : 2 * size]
    return turned


def attention_backward(
    width,
    query_ref,
    key_ref,
    value_ref,
    grad_ref,
    log_ref,
    window_ref,
    query_grad_ref,
    key_grad_ref,
    value_grad_ref,
    diagonal_ref,
    strip_ref,
    sums_ref,
    key_total,
    value_total,
):
    queries = query_ref.shape[0]
    keys = key_ref.shape[0]
    per_step = lane_count // width
    tiles = queries // lane_count
    lanes = lax.broadcasted_iota(jnp.int32, (1, lane_count), 1) // width
    rows = lax.broadcasted_iota(jnp.int32, (lane_count, 1), 0) // width
    keys_turned = key_ref[...].T
    for head in range(per_step):
        strip_ref[head] = bias_strip(window_ref[head])
    sums_ref[...] = jnp.zeros_like(sums_ref)
    key_total[...] = jnp.zeros_like(key_total)
    value_total[...] = jnp.zeros_like(value_total)
    for tile in range(tiles):
        span = pl.ds(tile * lane_count, lane_count)
        shifted = pl.ds((tiles - 1 - tile) * lane_count, keys)
        query_tile = query_ref[span, :]
        grad_tile = grad_ref[span, :]
        total = jnp.zeros((lane_count, lane_count), full)
        for head in range(per_step):
            own_query = jnp.where(lanes == head, query_tile, jnp.zeros_like(query_tile))
            own_grad = jnp.where(lanes == head, grad_tile, jnp.zeros_like(grad_tile))
            scores = dot_over(key_ref[...], own_query, 1, 1) + strip_ref[head, shifted, :]
            probs = jnp.exp(scores - log_ref[head, :, span])
            grad_probs = dot_over(value_ref[...], own_grad, 1, 1)
            weighted = probs * grad_probs
            delta = jnp.sum(weighted, axis=0, keepdims=True)
            grad_scores = (weighted - probs * delta).astype(low)
            sums_ref[head, shifted, :] += grad_scores.astype(full)
            value_total[...] += dot_over(probs.astype(low), own_grad, 1, 0)
            key_total[...] += dot_over(grad_scores, own_query, 1, 0)
            part = dot_over(keys_turned, grad_scores, 1, 0)
            total = jnp.where(rows == head, part, total)
        query_grad_ref[span, :] = total.T.astype(low)
    key_grad_ref[...] = key_total[...].astype(low)
    value_grad_ref[...] = value_total[...].astype(low)
    for head in range(per_step):
        diagonal_ref[head] = diagonal_fold(sums_ref[head], diagonal_ref.shape[2])


def forward_call(query_rows, keys_all, values_all, windows):
    queries, model_width = query_rows.shape
    keys = keys_all.shape[0]
    heads, _, span = windows.shape
    width = model_width // heads
    per_step = lane_count // width
    row_block = pl.BlockSpec((queries, lane_count), lambda h: (0, h))
    key_block = pl.BlockSpec((keys, lane_count), lambda h: (0, h))
    return pl.pallas_call(
        functools.partial(attention_forward, width),
        grid=(heads // per_step,),
        in_specs=[
            row_block,
            key_block,
            key_block,
            pl.BlockSpec((per_step, 1, span), lambda h: (h, 0, 0)),
        ],
        out_specs=[row_block, pl.BlockSpec((per_step, 1, queries), lambda h: (h, 0, 0))],
        out_shape=[
            jax.ShapeDtypeStruct((queries, model_width), low),
            jax.ShapeDtypeStruct((heads, 1, queries), full),
        ],
        scratch_shapes=[pltpu.VMEM((per_step, span - lane_count, lane_count), full)],
        compiler_params=pltpu.CompilerParams(vmem_limit_bytes=40 * 2**20),
        name="attention_forward",
    )(query_rows, keys_all, values_all, windows)


def backward_call(query_rows, keys_all, values_all, grad_rows, logs, windows):
    queries, model_width = query_rows.shape
    keys = keys_all.shape[0]
    heads, _, span = windows.shape
    width = model_width // heads
    per_step = lane_count // width
    row_block = pl.BlockSpec((queries, lane_count), lambda h: (0, h))
    key_block = pl.BlockSpec((keys, lane_count), lambda h: (0, h))
    window_block = pl.BlockSpec((per_step, 1, span), lambda h: (h, 0, 0))
    return pl.pallas_call(
        functools.partial(attention_backward, width),
        grid=(heads // per_step,),
        in_specs=[
            row_block,
            key_block,
            key_block,
            row_block,
            pl.BlockSpec((per_step, 1, queries), lambda h: (h, 0, 0)),
            window_block,
        ],
        out_specs=[row_block, key_block, key_block, window_block],
        out_shape=[
            jax.ShapeDtypeStruct((queries, model_width), low),
            jax.ShapeDtypeStruct((keys, model_width), low),
            jax.ShapeDtypeStruct((keys, model_width), low),
            jax.ShapeDtypeStruct((heads, 1, span), full),
        ],
        scratch_shapes=[
            pltpu.VMEM((per_step, span - lane_count, lane_count), full),
            pltpu.VMEM((per_step, span - lane_count, lane_count), full),
            pltpu.VMEM((keys, lane_count), full),
            pltpu.VMEM((keys, lane_count), full),
        ],
        compiler_params=pltpu.CompilerParams(vmem_limit_bytes=40 * 2**20),
        name="attention_backward",
    )(query_rows, keys_all, values_all, grad_rows, logs, windows)


def swap(values, axis, distance):
    size = lax.axis_size(axis)
    return lax.ppermute(values, axis, [(place, place ^ distance) for place in range(size)])


def paired():
    return lax.axis_size("context") == 2


def square_gather(piece):
    half = piece.shape[-1] // 2
    one = swap(piece, "fsdp", 1)
    two = swap(piece, "fsdp", 2)
    far = jnp.concatenate(
        (swap(two[..., :half], "fsdp", 1), swap(one[..., half:], "fsdp", 2)), axis=-1
    )
    return (piece, one, two, far)


def place_pieces(pieces, start, place):
    for distance, piece in enumerate(pieces):
        start = place(start, piece, lax.axis_index("fsdp") ^ distance)
    return start


def gather_rows(shard):
    if lax.axis_size("fsdp") != 4:
        return lax.all_gather(shard, "fsdp", axis=0, tiled=True)
    rows, columns = shard.shape
    if not paired():
        return place_pieces(
            square_gather(shard),
            jnp.zeros((4, rows, columns), shard.dtype),
            lambda whole, piece, owner: lax.dynamic_update_slice(whole, piece[None], (owner, 0, 0)),
        ).reshape(4 * rows, columns)
    core = lax.axis_index("context")
    half = rows // 2
    mine = square_gather(lax.dynamic_slice_in_dim(shard, core * half, half, 0))
    theirs = [swap(piece, "context", 1) for piece in mine]
    whole = jnp.zeros((4, 2, half, columns), shard.dtype)

    def place_at(side):
        return lambda whole, piece, owner: lax.dynamic_update_slice(
            whole, piece[None, None], (owner, side, 0, 0)
        )

    whole = place_pieces(mine, whole, place_at(core))
    whole = place_pieces(theirs, whole, place_at(1 - core))
    return whole.reshape(4 * rows, columns)


def gather_flat(vector):
    if lax.axis_size("fsdp") != 4:
        return lax.all_gather(vector, "fsdp", axis=0)
    row = lax.axis_index("fsdp")
    near = swap(vector, "fsdp", 1)
    pair = jnp.stack((vector, near))
    other = swap(pair, "fsdp", 2)
    whole = jnp.zeros((4,) + vector.shape, vector.dtype)
    for distance, piece in enumerate((pair[0], pair[1], other[0], other[1])):
        whole = lax.dynamic_update_slice(whole, piece[None], (row ^ distance, 0))
    return whole


def take(blocks, place):
    return lax.dynamic_index_in_dim(blocks, place, 0, keepdims=False)


def add_low(left, right):
    return (left.astype(full) + right.astype(full)).astype(low)


def square_scatter(blocks):
    row = lax.axis_index("fsdp")
    half = blocks.shape[-1] // 2
    results = []
    for part, (first, second) in ((blocks[..., :half], (1, 2)), (blocks[..., half:], (2, 1))):
        away = jnp.stack((take(part, row ^ first), take(part, row ^ 3)))
        came = swap(away, "fsdp", first)
        onward = add_low(take(part, row ^ second), came[1])
        kept = take(part, row).astype(full) + came[0].astype(full)
        results.append(kept + swap(onward, "fsdp", second).astype(full))
    return jnp.concatenate(results, axis=-1)


def scatter_half(grad):
    rows, columns = grad.shape
    core = lax.axis_index("context")
    blocks = grad.astype(low).reshape(4, 2, rows // 8, columns)

    def side(which):
        return lax.dynamic_index_in_dim(blocks, which, 1, keepdims=False)

    came = swap(side(1 - core), "context", 1)
    return square_scatter(add_low(side(core), came))


def join_cores(half):
    core = lax.axis_index("context")
    other = swap(half, "context", 1)
    whole = jnp.zeros((2,) + half.shape, half.dtype)
    whole = lax.dynamic_update_slice(whole, half[None], (core, 0, 0))
    whole = lax.dynamic_update_slice(whole, other[None], (1 - core, 0, 0))
    return whole.reshape(2 * half.shape[0], half.shape[1]).astype(full)


def sum_experts(share):
    size = lax.axis_size("expert")
    rows, columns = share.shape
    if size != 4 or rows % 64:
        return lax.psum(share, "expert")
    row = lax.axis_index("expert")
    blocks = share.astype(low).reshape(4, rows // 4, columns)
    own = take(blocks, row).astype(full)
    for distance in (1, 2, 3):
        own = own + swap(take(blocks, row ^ distance), "expert", distance).astype(full)
    own = own.astype(low)
    whole = lax.dynamic_update_slice(jnp.zeros_like(blocks), own[None], (row, 0, 0))
    for distance in (1, 2, 3):
        came = swap(own, "expert", distance)
        whole = lax.dynamic_update_slice(whole, came[None], (row ^ distance, 0, 0))
    return whole.reshape(rows, columns)


def dense_reduce(grad):
    if lax.axis_size("fsdp") == 4 and paired():
        half = scatter_half(grad)
        tall = half.reshape(-1, 768 if half.size % 768 == 0 else half.shape[1])
        return join_cores(sum_experts(tall).reshape(half.shape).astype(low))
    share = lax.psum_scatter(grad.astype(low), "fsdp", scatter_dimension=0, tiled=True)
    return lax.psum(share.astype(full), ("context", "expert"))


def expert_reduce(grad):
    if lax.axis_size("fsdp") == 4 and paired():
        return join_cores(scatter_half(grad).astype(low))
    share = lax.psum_scatter(grad.astype(low), "fsdp", scatter_dimension=0, tiled=True)
    return lax.psum(share, "context").astype(full)


def gather_positions(rows):
    if not paired():
        return lax.all_gather(rows, "context", axis=0, tiled=True)
    core = lax.axis_index("context")
    other = swap(rows, "context", 1)
    count = rows.shape[0]
    whole = jnp.zeros((2 * count,) + rows.shape[1:], rows.dtype)
    whole = lax.dynamic_update_slice(whole, rows, (core * count, 0))
    return lax.dynamic_update_slice(whole, other, ((1 - core) * count, 0))


def scatter_positions(rows):
    if not paired():
        return lax.psum_scatter(rows, "context", scatter_dimension=0, tiled=True)
    core = lax.axis_index("context")
    count = rows.shape[0] // 2
    came = swap(lax.dynamic_slice_in_dim(rows, (1 - core) * count, count, 0), "context", 1)
    return add_low(lax.dynamic_slice_in_dim(rows, core * count, count, 0), came)


def rms_norm(values, norm_gain):
    return (
        values * lax.rsqrt(jnp.mean(values * values, axis=-1, keepdims=True) + epsilon) * norm_gain
    )


def smooth(values):
    return jax.nn.gelu(values, approximate=True)


def per_device(
    tokens,
    cotangent,
    expert_ids,
    capacity_slot,
    buckets,
    attn_gain,
    query_weight,
    key_weight,
    value_weight,
    attention_output_matrix,
    bias_table,
    mixture_gain,
    router_matrix,
    expert_in,
    expert_out,
):
    row_count = tokens.shape[1]
    model_width = tokens.shape[2]
    inputs = tokens.reshape(row_count, model_width).astype(jnp.float32)
    upstream = cotangent.reshape(row_count, model_width).astype(jnp.float32)
    chosen = expert_ids.reshape(row_count)
    slot_ids = capacity_slot.reshape(row_count)
    seq_length = (buckets.shape[0] + 1) // 2
    gain_rows = attn_gain.shape[0]
    experts = router_matrix.shape[1]
    small = gather_flat(
        jnp.concatenate(
            (attn_gain, mixture_gain, router_matrix.reshape(-1), bias_table.reshape(-1))
        )
    )
    gain_one = small[:, :gain_rows].reshape(-1)
    gain_two = small[:, gain_rows : 2 * gain_rows].reshape(-1)
    w_router = small[:, 2 * gain_rows : (2 + experts) * gain_rows].reshape(-1, experts)
    table_rows = small[:, (2 + experts) * gain_rows :].reshape(-1, bias_table.shape[1])
    w_inner = gather_rows(jnp.concatenate((query_weight, key_weight, value_weight), axis=1))
    w_output = gather_rows(attention_output_matrix)
    w_first = gather_rows(expert_in[0])
    w_second = gather_rows(expert_out[0])
    head_count = table_rows.shape[1]
    head_dim = model_width // head_count
    bucket_count = table_rows.shape[0]
    normalized_input, norm_one_back = jax.vjp(rms_norm, inputs, gain_one.astype(jnp.float32))
    hidden = normalized_input.astype(jnp.bfloat16)
    inner = jnp.dot(hidden, w_inner, preferred_element_type=jnp.float32).astype(jnp.bfloat16)
    query_rows = inner[:, :model_width]
    pairs_all = gather_positions(inner[:, model_width:])
    keys_all = pairs_all[:, :model_width]
    values_all = pairs_all[:, model_width:]
    first_row = lax.axis_index("context") * row_count
    bucket_ids = jnp.arange(bucket_count, dtype=jnp.int32)
    window_start = seq_length - row_count - first_row
    window_buckets = lax.dynamic_slice_in_dim(
        jnp.pad(buckets, (0, 1)), window_start, row_count + seq_length, 0
    )
    offset_onehot = (window_buckets[:, None] == bucket_ids).astype(jnp.float32)
    windows = jnp.einsum(
        "ob,bh->ho", offset_onehot, table_rows.astype(jnp.float32), precision=highest_score
    )[:, None, :]
    attended_low, log_total = forward_call(query_rows, keys_all, values_all, windows)
    middle = inputs + jnp.dot(attended_low, w_output, preferred_element_type=jnp.float32)
    expert_groups = lax.axis_size("expert")
    capacity = row_count * 5 // (4 * experts)
    normed_two, norm_two_back = jax.vjp(rms_norm, middle, gain_two.astype(jnp.float32))
    second_hidden = normed_two.astype(jnp.bfloat16)
    router_logits = jnp.dot(second_hidden, w_router, preferred_element_type=jnp.float32)
    shifted = router_logits - jnp.max(router_logits, axis=-1, keepdims=True)
    raised = jnp.exp(shifted)
    router_probs = raised / jnp.sum(raised, axis=-1, keepdims=True)
    selector = (chosen[:, None] == jnp.arange(experts, dtype=jnp.int32)).astype(jnp.float32)
    gate_value = jnp.sum(router_probs * selector, axis=-1)
    position = chosen * capacity + slot_ids
    dispatch = (
        (position[:, None] == jnp.arange(experts * capacity, dtype=jnp.int32))
        & (slot_ids[:, None] >= 0)
    ).astype(jnp.bfloat16)
    outgoing = jnp.einsum("tc,td->cd", dispatch, second_hidden, preferred_element_type=jnp.float32)
    outgoing = outgoing.astype(jnp.bfloat16).reshape(
        expert_groups, capacity, model_width
    )
    received = lax.all_to_all(outgoing, "expert", split_axis=0, concat_axis=0, tiled=True)
    pre_act = jnp.einsum("scd,df->scf", received, w_first, preferred_element_type=jnp.float32)
    activated = smooth(pre_act).astype(jnp.bfloat16)
    produced = jnp.einsum(
        "scf,fd->scd", activated, w_second, preferred_element_type=jnp.float32
    ).astype(jnp.bfloat16)
    returned = lax.all_to_all(produced, "expert", split_axis=0, concat_axis=0, tiled=True)
    combined = jnp.einsum(
        "tc,cd->td",
        dispatch,
        returned.reshape(experts * capacity, model_width),
        preferred_element_type=jnp.float32,
    )
    layer_sum = middle + gate_value[:, None] * combined
    grad_gate = jnp.sum(upstream * combined, axis=-1)
    weighted_grad = (gate_value[:, None] * upstream).astype(jnp.bfloat16)
    grad_slots = jnp.einsum(
        "tc,td->cd", dispatch, weighted_grad, preferred_element_type=jnp.float32
    )
    grad_slots = grad_slots.astype(jnp.bfloat16).reshape(
        expert_groups, capacity, model_width
    )
    grad_produced = lax.all_to_all(grad_slots, "expert", split_axis=0, concat_axis=0, tiled=True)
    grad_act = jnp.einsum(
        "scd,fd->scf", grad_produced, w_second, preferred_element_type=jnp.float32
    )
    activated_again, smooth_back = jax.vjp(smooth, pre_act)
    grad_pre = smooth_back(grad_act)[0].astype(jnp.bfloat16)
    second_grad = jnp.einsum(
        "scf,scd->fd",
        activated_again.astype(jnp.bfloat16),
        grad_produced,
        preferred_element_type=jnp.float32,
    )
    first_grad = jnp.einsum(
        "scd,scf->df", received, grad_pre, preferred_element_type=jnp.float32
    )
    grad_received = jnp.einsum(
        "scf,df->scd", grad_pre, w_first, preferred_element_type=jnp.float32
    ).astype(jnp.bfloat16)
    grad_sent = lax.all_to_all(grad_received, "expert", split_axis=0, concat_axis=0, tiled=True)
    grad_hidden_two = jnp.einsum(
        "tc,cd->td",
        dispatch,
        grad_sent.reshape(experts * capacity, model_width),
        preferred_element_type=jnp.float32,
    )
    grad_logits = router_probs * (selector - gate_value[:, None]) * grad_gate[:, None]
    router_grad = jnp.einsum(
        "td,te->de", second_hidden.astype(jnp.float32), grad_logits, precision=highest_score
    )
    grad_hidden_two = grad_hidden_two + jnp.einsum(
        "te,de->td", grad_logits, w_router.astype(jnp.float32), precision=highest_score
    )
    grad_middle_norm, gain_two_grad = norm_two_back(grad_hidden_two)
    grad_middle = upstream + grad_middle_norm
    grad_branch = grad_middle.astype(jnp.bfloat16)
    output_grad = jnp.einsum(
        "td,te->de", attended_low, grad_branch, preferred_element_type=jnp.float32
    )
    grad_attended = jnp.einsum(
        "te,de->td", grad_branch, w_output, preferred_element_type=jnp.float32
    ).astype(jnp.bfloat16)
    grad_query_low, key_terms, value_terms, diagonals = backward_call(
        query_rows, keys_all, values_all, grad_attended, log_total, windows
    )
    table_grad = jnp.einsum(
        "hw,wb->bh", diagonals[:, 0, :], offset_onehot, precision=highest_score
    )
    pair_grad = scatter_positions(jnp.concatenate((key_terms, value_terms), axis=1))
    inner_grad = jnp.concatenate((grad_query_low, pair_grad), axis=1)
    inner_share = dense_reduce(
        jnp.einsum("td,te->de", hidden, inner_grad, preferred_element_type=jnp.float32)
    )
    grad_hidden = jnp.einsum("te,de->td", inner_grad, w_inner, preferred_element_type=jnp.float32)
    grad_inputs_norm, gain_one_grad = norm_one_back(grad_hidden)
    tokens_grad = (grad_middle + grad_inputs_norm).astype(jnp.bfloat16).reshape(tokens.shape)
    layer_out = layer_sum.astype(jnp.bfloat16).reshape(tokens.shape)
    fsdp_size = lax.axis_size("fsdp")
    small_sum = lax.psum(
        jnp.concatenate(
            [
                term.reshape(fsdp_size, -1)
                for term in (gain_one_grad, gain_two_grad, router_grad, table_grad)
            ],
            axis=1,
        ),
        ("fsdp", "context", "expert"),
    )
    small_share = take(small_sum, lax.axis_index("fsdp"))
    output_share = dense_reduce(output_grad)
    return (
        layer_out,
        tokens_grad,
        small_share[:gain_rows],
        inner_share[:, :model_width],
        inner_share[:, model_width : 2 * model_width],
        inner_share[:, 2 * model_width :],
        output_share,
        small_share[(2 + experts) * gain_rows :].reshape(bias_table.shape),
        small_share[gain_rows : 2 * gain_rows],
        small_share[2 * gain_rows : (2 + experts) * gain_rows].reshape(router_matrix.shape),
        expert_reduce(first_grad)[None],
        expert_reduce(second_grad)[None],
    )


def solution(mesh):
    return jax.shard_map(
        per_device,
        mesh=mesh,
        in_specs=(
            P(("fsdp", "expert"), "context", None),
            P(("fsdp", "expert"), "context", None),
            P(("fsdp", "expert"), "context"),
            P(("fsdp", "expert"), "context"),
            P(),
            P("fsdp"),
            P("fsdp", None),
            P("fsdp", None),
            P("fsdp", None),
            P("fsdp", None),
            P("fsdp", None),
            P("fsdp"),
            P("fsdp", None),
            P("expert", "fsdp", None),
            P("expert", "fsdp", None),
        ),
        out_specs=(
            P(("fsdp", "expert"), "context", None),
            P(("fsdp", "expert"), "context", None),
            P("fsdp"),
            P("fsdp", None),
            P("fsdp", None),
            P("fsdp", None),
            P("fsdp", None),
            P("fsdp", None),
            P("fsdp"),
            P("fsdp", None),
            P("expert", "fsdp", None),
            P("expert", "fsdp", None),
        ),
        check_vma=False,
    )
```

```python
import functools

import jax
import jax.numpy as jnp
from jax import lax
from jax.experimental import pallas as pl
from jax.experimental.pallas import tpu as pltpu
from jax.sharding import PartitionSpec as P

highest_score = lax.Precision.HIGHEST
epsilon = 1e-06
low = jnp.bfloat16
full = jnp.float32
lane_count = 128


def dot_over(left, right, left_dim, right_dim):
    return lax.dot_general(
        left, right, (((left_dim,), (right_dim,)), ((), ())), preferred_element_type=full
    )


def bias_strip(window):
    width = window.shape[1]
    spread = jnp.broadcast_to(window, (lane_count, width))
    rolled = pltpu.roll(spread, width - lane_count + 1, 1, stride=1, stride_axis=0)
    return rolled[:, : width - lane_count].T


def attention_forward(width, query_ref, key_ref, value_ref, window_ref, out_ref, log_ref, strip_ref):
    queries = query_ref.shape[0]
    keys = key_ref.shape[0]
    per_step = lane_count // width
    tiles = queries // lane_count
    lanes = lax.broadcasted_iota(jnp.int32, (1, lane_count), 1) // width
    rows = lax.broadcasted_iota(jnp.int32, (lane_count, 1), 0) // width
    values_turned = value_ref[...].T
    for head in range(per_step):
        strip_ref[head] = bias_strip(window_ref[head])
    for tile in range(tiles):
        span = pl.ds(tile * lane_count, lane_count)
        query_tile = query_ref[span, :]
        total = jnp.zeros((lane_count, lane_count), full)
        for head in range(per_step):
            own = jnp.where(lanes == head, query_tile, jnp.zeros_like(query_tile))
            scores = dot_over(key_ref[...], own, 1, 1)
            scores = scores + strip_ref[head, pl.ds((tiles - 1 - tile) * lane_count, keys), :]
            top = jnp.max(scores, axis=0, keepdims=True)
            raised = jnp.exp(scores - top)
            summed = jnp.sum(raised, axis=0, keepdims=True)
            log_ref[head, :, span] = top + jnp.log(summed)
            part = dot_over(values_turned, raised.astype(low), 1, 0) / summed
            total = jnp.where(rows == head, part, total)
        out_ref[span, :] = total.T.astype(low)


def diagonal_fold(strip_sum, window_width):
    turned = strip_sum.T
    turned = jnp.concatenate(
        (turned, jnp.zeros((lane_count, window_width - turned.shape[1]), full)), axis=1
    )
    size = lane_count
    while size > 1:
        size //= 2
        turned = pltpu.roll(turned[:size], size, 1) + turned[size : 2 * size]
    return turned


def attention_backward(
    width,
    query_ref,
    key_ref,
    value_ref,
    grad_ref,
    log_ref,
    window_ref,
    query_grad_ref,
    key_grad_ref,
    value_grad_ref,
    diagonal_ref,
    strip_ref,
    sums_ref,
    key_total,
    value_total,
):
    queries = query_ref.shape[0]
    keys = key_ref.shape[0]
    per_step = lane_count // width
    tiles = queries // lane_count
    lanes = lax.broadcasted_iota(jnp.int32, (1, lane_count), 1) // width
    rows = lax.broadcasted_iota(jnp.int32, (lane_count, 1), 0) // width
    keys_turned = key_ref[...].T
    for head in range(per_step):
        strip_ref[head] = bias_strip(window_ref[head])
    sums_ref[...] = jnp.zeros_like(sums_ref)
    key_total[...] = jnp.zeros_like(key_total)
    value_total[...] = jnp.zeros_like(value_total)
    for tile in range(tiles):
        span = pl.ds(tile * lane_count, lane_count)
        shifted = pl.ds((tiles - 1 - tile) * lane_count, keys)
        query_tile = query_ref[span, :]
        grad_tile = grad_ref[span, :]
        total = jnp.zeros((lane_count, lane_count), full)
        for head in range(per_step):
            own_query = jnp.where(lanes == head, query_tile, jnp.zeros_like(query_tile))
            own_grad = jnp.where(lanes == head, grad_tile, jnp.zeros_like(grad_tile))
            scores = dot_over(key_ref[...], own_query, 1, 1) + strip_ref[head, shifted, :]
            probs = jnp.exp(scores - log_ref[head, :, span])
            grad_probs = dot_over(value_ref[...], own_grad, 1, 1)
            weighted = probs * grad_probs
            delta = jnp.sum(weighted, axis=0, keepdims=True)
            grad_scores = (weighted - probs * delta).astype(low)
            sums_ref[head, shifted, :] += grad_scores.astype(full)
            value_total[...] += dot_over(probs.astype(low), own_grad, 1, 0)
            key_total[...] += dot_over(grad_scores, own_query, 1, 0)
            part = dot_over(keys_turned, grad_scores, 1, 0)
            total = jnp.where(rows == head, part, total)
        query_grad_ref[span, :] = total.T.astype(low)
    key_grad_ref[...] = key_total[...].astype(low)
    value_grad_ref[...] = value_total[...].astype(low)
    for head in range(per_step):
        diagonal_ref[head] = diagonal_fold(sums_ref[head], diagonal_ref.shape[2])


def forward_call(query_rows, keys_all, values_all, windows):
    queries, model_width = query_rows.shape
    keys = keys_all.shape[0]
    heads, _, span = windows.shape
    width = model_width // heads
    per_step = lane_count // width
    row_block = pl.BlockSpec((queries, lane_count), lambda h: (0, h))
    key_block = pl.BlockSpec((keys, lane_count), lambda h: (0, h))
    return pl.pallas_call(
        functools.partial(attention_forward, width),
        grid=(heads // per_step,),
        in_specs=[
            row_block,
            key_block,
            key_block,
            pl.BlockSpec((per_step, 1, span), lambda h: (h, 0, 0)),
        ],
        out_specs=[row_block, pl.BlockSpec((per_step, 1, queries), lambda h: (h, 0, 0))],
        out_shape=[
            jax.ShapeDtypeStruct((queries, model_width), low),
            jax.ShapeDtypeStruct((heads, 1, queries), full),
        ],
        scratch_shapes=[pltpu.VMEM((per_step, span - lane_count, lane_count), full)],
        compiler_params=pltpu.CompilerParams(vmem_limit_bytes=40 * 2**20),
        name="attention_forward",
    )(query_rows, keys_all, values_all, windows)


def backward_call(query_rows, keys_all, values_all, grad_rows, logs, windows):
    queries, model_width = query_rows.shape
    keys = keys_all.shape[0]
    heads, _, span = windows.shape
    width = model_width // heads
    per_step = lane_count // width
    row_block = pl.BlockSpec((queries, lane_count), lambda h: (0, h))
    key_block = pl.BlockSpec((keys, lane_count), lambda h: (0, h))
    window_block = pl.BlockSpec((per_step, 1, span), lambda h: (h, 0, 0))
    return pl.pallas_call(
        functools.partial(attention_backward, width),
        grid=(heads // per_step,),
        in_specs=[
            row_block,
            key_block,
            key_block,
            row_block,
            pl.BlockSpec((per_step, 1, queries), lambda h: (h, 0, 0)),
            window_block,
        ],
        out_specs=[row_block, key_block, key_block, window_block],
        out_shape=[
            jax.ShapeDtypeStruct((queries, model_width), low),
            jax.ShapeDtypeStruct((keys, model_width), low),
            jax.ShapeDtypeStruct((keys, model_width), low),
            jax.ShapeDtypeStruct((heads, 1, span), full),
        ],
        scratch_shapes=[
            pltpu.VMEM((per_step, span - lane_count, lane_count), full),
            pltpu.VMEM((per_step, span - lane_count, lane_count), full),
            pltpu.VMEM((keys, lane_count), full),
            pltpu.VMEM((keys, lane_count), full),
        ],
        compiler_params=pltpu.CompilerParams(vmem_limit_bytes=40 * 2**20),
        name="attention_backward",
    )(query_rows, keys_all, values_all, grad_rows, logs, windows)


def swap(values, axis, distance):
    size = lax.axis_size(axis)
    return lax.ppermute(values, axis, [(place, place ^ distance) for place in range(size)])


def paired():
    return lax.axis_size("context") == 2


def square_gather(piece):
    half = piece.shape[-1] // 2
    one = swap(piece, "fsdp", 1)
    two = swap(piece, "fsdp", 2)
    far = jnp.concatenate(
        (swap(two[..., :half], "fsdp", 1), swap(one[..., half:], "fsdp", 2)), axis=-1
    )
    return (piece, one, two, far)


def place_pieces(pieces, start, place):
    for distance, piece in enumerate(pieces):
        start = place(start, piece, lax.axis_index("fsdp") ^ distance)
    return start


def gather_rows(shard):
    if lax.axis_size("fsdp") != 4:
        return lax.all_gather(shard, "fsdp", axis=0, tiled=True)
    rows, columns = shard.shape
    if not paired():
        return place_pieces(
            square_gather(shard),
            jnp.zeros((4, rows, columns), shard.dtype),
            lambda whole, piece, owner: lax.dynamic_update_slice(whole, piece[None], (owner, 0, 0)),
        ).reshape(4 * rows, columns)
    core = lax.axis_index("context")
    half = rows // 2
    mine = square_gather(lax.dynamic_slice_in_dim(shard, core * half, half, 0))
    theirs = [swap(piece, "context", 1) for piece in mine]
    return assemble(mine, theirs).reshape(4 * rows, columns)


def assemble_copies(*refs):
    piece_refs, whole_ref, arrived = refs[:8], refs[8], refs[9]
    row = lax.axis_index("fsdp")
    core = lax.axis_index("context")
    copies = [
        pltpu.make_async_copy(
            piece_refs[4 * side + distance],
            whole_ref.at[row ^ distance, (1 - core) if side else core],
            arrived.at[4 * side + distance],
        )
        for side in range(2)
        for distance in range(4)
    ]
    for copy in copies:
        copy.start()
    for copy in copies:
        copy.wait()


def assemble(mine, theirs):
    half, columns = mine[0].shape
    return pl.pallas_call(
        assemble_copies,
        in_specs=[pl.BlockSpec(memory_space=pl.ANY)] * 8,
        out_specs=pl.BlockSpec(memory_space=pl.ANY),
        out_shape=jax.ShapeDtypeStruct((4, 2, half, columns), mine[0].dtype),
        scratch_shapes=[pltpu.SemaphoreType.DMA((8,))],
        name="assemble",
    )(*mine, *theirs)


def small_reduce(terms):
    row = lax.axis_index("fsdp")
    if lax.axis_size("fsdp") != 4 or not paired() or lax.axis_size("expert") != 4:
        return take(lax.psum(terms, ("fsdp", "context", "expert")), row)
    came = swap(jnp.stack((take(terms, row ^ 1), take(terms, row ^ 3))), "fsdp", 1)
    own = take(terms, row) + came[0] + swap(take(terms, row ^ 2) + came[1], "fsdp", 2)
    own = own + swap(own, "context", 1)
    own = own + swap(own, "expert", 1)
    return own + swap(own, "expert", 2)


def gather_flat(vector):
    if lax.axis_size("fsdp") != 4:
        return lax.all_gather(vector, "fsdp", axis=0)
    row = lax.axis_index("fsdp")
    near = swap(vector, "fsdp", 1)
    pair = jnp.stack((vector, near))
    other = swap(pair, "fsdp", 2)
    whole = jnp.zeros((4,) + vector.shape, vector.dtype)
    for distance, piece in enumerate((pair[0], pair[1], other[0], other[1])):
        whole = lax.dynamic_update_slice(whole, piece[None], (row ^ distance, 0))
    return whole


def take(blocks, place):
    return lax.dynamic_index_in_dim(blocks, place, 0, keepdims=False)


def add_low(left, right):
    return (left.astype(full) + right.astype(full)).astype(low)


def square_scatter(blocks):
    row = lax.axis_index("fsdp")
    half = blocks.shape[-1] // 2
    results = []
    for part, (first, second) in ((blocks[..., :half], (1, 2)), (blocks[..., half:], (2, 1))):
        away = jnp.stack((take(part, row ^ first), take(part, row ^ 3)))
        came = swap(away, "fsdp", first)
        onward = add_low(take(part, row ^ second), came[1])
        kept = take(part, row).astype(full) + came[0].astype(full)
        results.append(kept + swap(onward, "fsdp", second).astype(full))
    return jnp.concatenate(results, axis=-1)


def scatter_half(grad):
    rows, columns = grad.shape
    core = lax.axis_index("context")
    blocks = grad.astype(low).reshape(4, 2, rows // 8, columns)

    def side(which):
        return lax.dynamic_index_in_dim(blocks, which, 1, keepdims=False)

    came = swap(side(1 - core), "context", 1)
    return square_scatter(add_low(side(core), came))


def join_cores(half):
    core = lax.axis_index("context")
    other = swap(half, "context", 1)
    whole = jnp.zeros((2,) + half.shape, half.dtype)
    whole = lax.dynamic_update_slice(whole, half[None], (core, 0, 0))
    whole = lax.dynamic_update_slice(whole, other[None], (1 - core, 0, 0))
    return whole.reshape(2 * half.shape[0], half.shape[1]).astype(full)


def sum_experts(share):
    size = lax.axis_size("expert")
    rows, columns = share.shape
    if size != 4 or rows % 4:
        return lax.psum(share, "expert")
    row = lax.axis_index("expert")
    blocks = share.astype(low).reshape(4, rows // 4, columns)
    own = take(blocks, row).astype(full)
    for distance in (1, 2, 3):
        own = own + swap(take(blocks, row ^ distance), "expert", distance).astype(full)
    own = own.astype(low)
    whole = lax.dynamic_update_slice(jnp.zeros_like(blocks), own[None], (row, 0, 0))
    for distance in (1, 2, 3):
        came = swap(own, "expert", distance)
        whole = lax.dynamic_update_slice(whole, came[None], (row ^ distance, 0, 0))
    return whole.reshape(rows, columns)


def dense_reduce(grad):
    if lax.axis_size("fsdp") == 4 and paired():
        half = scatter_half(grad)
        tall = half.reshape(-1, 768 if half.size % 768 == 0 else half.shape[1])
        return join_cores(sum_experts(tall).reshape(half.shape).astype(low))
    share = lax.psum_scatter(grad.astype(low), "fsdp", scatter_dimension=0, tiled=True)
    return lax.psum(share.astype(full), ("context", "expert"))


def expert_reduce(grad):
    if lax.axis_size("fsdp") == 4 and paired():
        return join_cores(scatter_half(grad).astype(low))
    share = lax.psum_scatter(grad.astype(low), "fsdp", scatter_dimension=0, tiled=True)
    return lax.psum(share, "context").astype(full)


def gather_positions(rows):
    if not paired():
        return lax.all_gather(rows, "context", axis=0, tiled=True)
    core = lax.axis_index("context")
    other = swap(rows, "context", 1)
    count = rows.shape[0]
    whole = jnp.zeros((2 * count,) + rows.shape[1:], rows.dtype)
    whole = lax.dynamic_update_slice(whole, rows, (core * count, 0))
    return lax.dynamic_update_slice(whole, other, ((1 - core) * count, 0))


def scatter_positions(rows):
    if not paired():
        return lax.psum_scatter(rows, "context", scatter_dimension=0, tiled=True)
    core = lax.axis_index("context")
    count = rows.shape[0] // 2
    came = swap(lax.dynamic_slice_in_dim(rows, (1 - core) * count, count, 0), "context", 1)
    return add_low(lax.dynamic_slice_in_dim(rows, core * count, count, 0), came)


def rms_norm(values, norm_gain):
    return (
        values * lax.rsqrt(jnp.mean(values * values, axis=-1, keepdims=True) + epsilon) * norm_gain
    )


def smooth(values):
    return jax.nn.gelu(values, approximate=True)


def per_device(
    tokens,
    cotangent,
    expert_ids,
    capacity_slot,
    buckets,
    attn_gain,
    query_weight,
    key_weight,
    value_weight,
    attention_output_matrix,
    bias_table,
    mixture_gain,
    router_matrix,
    expert_in,
    expert_out,
):
    row_count = tokens.shape[1]
    model_width = tokens.shape[2]
    inputs = tokens.reshape(row_count, model_width).astype(jnp.float32)
    upstream = cotangent.reshape(row_count, model_width).astype(jnp.float32)
    chosen = expert_ids.reshape(row_count)
    slot_ids = capacity_slot.reshape(row_count)
    seq_length = (buckets.shape[0] + 1) // 2
    gain_rows = attn_gain.shape[0]
    experts = router_matrix.shape[1]
    small = gather_flat(
        jnp.concatenate(
            (attn_gain, mixture_gain, router_matrix.reshape(-1), bias_table.reshape(-1))
        )
    )
    gain_one = small[:, :gain_rows].reshape(-1)
    gain_two = small[:, gain_rows : 2 * gain_rows].reshape(-1)
    w_router = small[:, 2 * gain_rows : (2 + experts) * gain_rows].reshape(-1, experts)
    table_rows = small[:, (2 + experts) * gain_rows :].reshape(-1, bias_table.shape[1])
    w_inner = gather_rows(jnp.concatenate((query_weight, key_weight, value_weight), axis=1))
    w_inner, output_shard, first_shard, second_shard = lax.optimization_barrier(
        (w_inner, attention_output_matrix, expert_in[0], expert_out[0])
    )
    w_output = gather_rows(output_shard)
    w_first = gather_rows(first_shard)
    w_second = gather_rows(second_shard)
    head_count = table_rows.shape[1]
    head_dim = model_width // head_count
    bucket_count = table_rows.shape[0]
    normalized_input, norm_one_back = jax.vjp(rms_norm, inputs, gain_one.astype(jnp.float32))
    hidden = normalized_input.astype(jnp.bfloat16)
    inner = jnp.dot(hidden, w_inner, preferred_element_type=jnp.float32).astype(jnp.bfloat16)
    query_rows = inner[:, :model_width]
    pairs_all = gather_positions(inner[:, model_width:])
    keys_all = pairs_all[:, :model_width]
    values_all = pairs_all[:, model_width:]
    first_row = lax.axis_index("context") * row_count
    bucket_ids = jnp.arange(bucket_count, dtype=jnp.int32)
    window_start = seq_length - row_count - first_row
    window_buckets = lax.dynamic_slice_in_dim(
        jnp.pad(buckets, (0, 1)), window_start, row_count + seq_length, 0
    )
    offset_onehot = (window_buckets[:, None] == bucket_ids).astype(jnp.float32)
    windows = jnp.einsum(
        "ob,bh->ho", offset_onehot, table_rows.astype(jnp.float32), precision=highest_score
    )[:, None, :]
    attended_low, log_total = forward_call(query_rows, keys_all, values_all, windows)
    middle = inputs + jnp.dot(attended_low, w_output, preferred_element_type=jnp.float32)
    expert_groups = lax.axis_size("expert")
    capacity = row_count * 5 // (4 * experts)
    normed_two, norm_two_back = jax.vjp(rms_norm, middle, gain_two.astype(jnp.float32))
    second_hidden = normed_two.astype(jnp.bfloat16)
    router_logits = jnp.dot(second_hidden, w_router, preferred_element_type=jnp.float32)
    shifted = router_logits - jnp.max(router_logits, axis=-1, keepdims=True)
    raised = jnp.exp(shifted)
    router_probs = raised / jnp.sum(raised, axis=-1, keepdims=True)
    selector = (chosen[:, None] == jnp.arange(experts, dtype=jnp.int32)).astype(jnp.float32)
    gate_value = jnp.sum(router_probs * selector, axis=-1)
    position = chosen * capacity + slot_ids
    dispatch = (
        (position[:, None] == jnp.arange(experts * capacity, dtype=jnp.int32))
        & (slot_ids[:, None] >= 0)
    ).astype(jnp.bfloat16)
    outgoing = jnp.einsum("tc,td->cd", dispatch, second_hidden, preferred_element_type=jnp.float32)
    outgoing = outgoing.astype(jnp.bfloat16).reshape(
        expert_groups, capacity, model_width
    )
    received = lax.all_to_all(outgoing, "expert", split_axis=0, concat_axis=0, tiled=True)
    pre_act = jnp.einsum("scd,df->scf", received, w_first, preferred_element_type=jnp.float32)
    activated = smooth(pre_act).astype(jnp.bfloat16)
    produced = jnp.einsum(
        "scf,fd->scd", activated, w_second, preferred_element_type=jnp.float32
    ).astype(jnp.bfloat16)
    returned = lax.all_to_all(produced, "expert", split_axis=0, concat_axis=0, tiled=True)
    combined = jnp.einsum(
        "tc,cd->td",
        dispatch,
        returned.reshape(experts * capacity, model_width),
        preferred_element_type=jnp.float32,
    )
    layer_sum = middle + gate_value[:, None] * combined
    grad_gate = jnp.sum(upstream * combined, axis=-1)
    weighted_grad = (gate_value[:, None] * upstream).astype(jnp.bfloat16)
    grad_slots = jnp.einsum(
        "tc,td->cd", dispatch, weighted_grad, preferred_element_type=jnp.float32
    )
    grad_slots = grad_slots.astype(jnp.bfloat16).reshape(
        expert_groups, capacity, model_width
    )
    grad_produced = lax.all_to_all(grad_slots, "expert", split_axis=0, concat_axis=0, tiled=True)
    grad_act = jnp.einsum(
        "scd,fd->scf", grad_produced, w_second, preferred_element_type=jnp.float32
    )
    activated_again, smooth_back = jax.vjp(smooth, pre_act)
    grad_pre = smooth_back(grad_act)[0].astype(jnp.bfloat16)
    second_grad = jnp.einsum(
        "scf,scd->fd",
        activated_again.astype(jnp.bfloat16),
        grad_produced,
        preferred_element_type=jnp.float32,
    )
    first_grad = jnp.einsum(
        "scd,scf->df", received, grad_pre, preferred_element_type=jnp.float32
    )
    grad_received = jnp.einsum(
        "scf,df->scd", grad_pre, w_first, preferred_element_type=jnp.float32
    ).astype(jnp.bfloat16)
    grad_sent = lax.all_to_all(grad_received, "expert", split_axis=0, concat_axis=0, tiled=True)
    grad_hidden_two = jnp.einsum(
        "tc,cd->td",
        dispatch,
        grad_sent.reshape(experts * capacity, model_width),
        preferred_element_type=jnp.float32,
    )
    grad_logits = router_probs * (selector - gate_value[:, None]) * grad_gate[:, None]
    router_grad = jnp.einsum(
        "td,te->de", second_hidden.astype(jnp.float32), grad_logits, precision=highest_score
    )
    grad_hidden_two = grad_hidden_two + jnp.einsum(
        "te,de->td", grad_logits, w_router.astype(jnp.float32), precision=highest_score
    )
    grad_middle_norm, gain_two_grad = norm_two_back(grad_hidden_two)
    grad_middle = upstream + grad_middle_norm
    grad_branch = grad_middle.astype(jnp.bfloat16)
    output_grad = jnp.einsum(
        "td,te->de", attended_low, grad_branch, preferred_element_type=jnp.float32
    )
    grad_attended = jnp.einsum(
        "te,de->td", grad_branch, w_output, preferred_element_type=jnp.float32
    ).astype(jnp.bfloat16)
    grad_query_low, key_terms, value_terms, diagonals = backward_call(
        query_rows, keys_all, values_all, grad_attended, log_total, windows
    )
    table_grad = jnp.einsum(
        "hw,wb->bh", diagonals[:, 0, :], offset_onehot, precision=highest_score
    )
    pair_grad = scatter_positions(jnp.concatenate((key_terms, value_terms), axis=1))
    inner_grad = jnp.concatenate((grad_query_low, pair_grad), axis=1)
    inner_share = dense_reduce(
        jnp.einsum("td,te->de", hidden, inner_grad, preferred_element_type=jnp.float32)
    )
    grad_hidden = jnp.einsum("te,de->td", inner_grad, w_inner, preferred_element_type=jnp.float32)
    grad_inputs_norm, gain_one_grad = norm_one_back(grad_hidden)
    tokens_grad = (grad_middle + grad_inputs_norm).astype(jnp.bfloat16).reshape(tokens.shape)
    layer_out = layer_sum.astype(jnp.bfloat16).reshape(tokens.shape)
    fsdp_size = lax.axis_size("fsdp")
    small_share = small_reduce(
        jnp.concatenate(
            [
                term.reshape(fsdp_size, -1)
                for term in (gain_one_grad, gain_two_grad, router_grad, table_grad)
            ],
            axis=1,
        )
    )
    output_share = dense_reduce(output_grad)
    return (
        layer_out,
        tokens_grad,
        small_share[:gain_rows],
        inner_share[:, :model_width],
        inner_share[:, model_width : 2 * model_width],
        inner_share[:, 2 * model_width :],
        output_share,
        small_share[(2 + experts) * gain_rows :].reshape(bias_table.shape),
        small_share[gain_rows : 2 * gain_rows],
        small_share[2 * gain_rows : (2 + experts) * gain_rows].reshape(router_matrix.shape),
        expert_reduce(first_grad)[None],
        expert_reduce(second_grad)[None],
    )


def solution(mesh):
    return jax.shard_map(
        per_device,
        mesh=mesh,
        in_specs=(
            P(("fsdp", "expert"), "context", None),
            P(("fsdp", "expert"), "context", None),
            P(("fsdp", "expert"), "context"),
            P(("fsdp", "expert"), "context"),
            P(),
            P("fsdp"),
            P("fsdp", None),
            P("fsdp", None),
            P("fsdp", None),
            P("fsdp", None),
            P("fsdp", None),
            P("fsdp"),
            P("fsdp", None),
            P("expert", "fsdp", None),
            P("expert", "fsdp", None),
        ),
        out_specs=(
            P(("fsdp", "expert"), "context", None),
            P(("fsdp", "expert"), "context", None),
            P("fsdp"),
            P("fsdp", None),
            P("fsdp", None),
            P("fsdp", None),
            P("fsdp", None),
            P("fsdp", None),
            P("fsdp"),
            P("fsdp", None),
            P("expert", "fsdp", None),
            P("expert", "fsdp", None),
        ),
        check_vma=False,
    )
```
